128 devices in a mesh: grp: 8 (over z, y_hi), blk: 16 (over y_lo, x, core).
Axes of the slice: x: 4, y: 4 (y_hi: 2, y_lo: 2; y = y_hi * 2 + y_lo), z: 4, core: 2. Of those that a mesh axis runs over, the one named last changes fastest.
Arguments:
- images: bfloat16 [131072, 1152], P(('grp', 'blk')), may hold values from -0.19921875 to 0.19921875
- texts: bfloat16 [131072, 1152], P(('grp', 'blk')), may hold values from -0.19921875 to 0.19921875
- log_logit_scale: float32 [1], replicated, may hold values from 1 to 2
- bias: float32 [1], replicated, may hold values from -3 to -1
Outputs:
- image_grad: float32 [131072, 1152], P(('grp', 'blk'))
- text_grad: float32 [131072, 1152], P(('grp', 'blk'))
The draws below stay inside these ranges and needn't reach their ends.
All inputs are finite; a program needn't handle non-finite values.
Results may differ from the reference program's by a relative error of at most 0.0041.
Values may be sent and summed in bfloat16 or wider, within the bound.
No kernel may reach another device: no remote copies, remote signals or barrier semaphores. Data moves between devices by JAX's collectives and lax.ppermute only.
A program may use at most 128 MiB of HBM per device.

```python
import jax
import jax.numpy as jnp
from jax import lax

D = 1152
ROWS = 1024
BATCH = 131072
N_GRP = 8
N_BLK = 16


def shard_levels(own_key, dims, split, least, high):
    def one(axis_at, shards_of):
        draws = jax.random.uniform(jax.random.fold_in(jax.random.fold_in(own_key, 6), axis_at), (shards_of,), jnp.float32, least / len(split), high / len(split))
        return jnp.repeat(jnp.exp(draws), dims[axis_at] // shards_of).reshape((-1,) + (1,) * (len(dims) - axis_at - 1))

    gain = one(*split[0])
    for cut in split[1:]:
        gain = gain * one(*cut)
    return gain


def noise(own_key, shape, scale, most, cuts=(), kind=jnp.bfloat16):
    array = scale * jax.random.normal(own_key, shape, jnp.float32)
    if cuts:
        array = array * shard_levels(own_key, shape, cuts, -0.22, 0.18)
    return jnp.clip(array, -most, most).astype(kind)


def setup_inputs(seed: int = 0) -> dict:
    seeds = jax.random.split(jax.random.key(seed), 5)
    images = noise(seeds[0], (BATCH, D), 0.03, 0.19921875, ((0, 128),))
    texts = noise(seeds[1], (BATCH, D), 0.03, 0.19921875, ((0, 128),))
    log_logit_scale = jnp.clip(jax.random.uniform(seeds[2], (1,), jnp.float32, 1.0, 2.0), 1.0, 2.0)
    bias = jnp.clip(jax.random.uniform(seeds[3], (1,), jnp.float32, -3.0, -1.0), -3.0, -1.0)
    return {"images": images, "texts": texts, "log_logit_scale": log_logit_scale, "bias": bias}


EPSILON = 1e-06

def unit_rows(raw):
    values = raw.astype(jnp.float32)
    norms = jnp.sqrt(lax.optimization_barrier(jnp.sum(values * values, axis=-1, keepdims=True)) + EPSILON)
    return (values / norms, norms)

def reference(images, texts, log_logit_scale, bias):
    scale_factor = jnp.exp(log_logit_scale[0])
    block_distance = bias[0]
    image_unit, image_norm = unit_rows(images)
    text_unit, text_norm = unit_rows(texts)
    image_lower_half = image_unit.astype(jnp.bfloat16).reshape(N_GRP, N_BLK, ROWS, D)
    text_lower_half = text_unit.astype(jnp.bfloat16).reshape(N_GRP, N_BLK, ROWS, D)
    image_full_width = image_lower_half.astype(jnp.float32)
    identity = jnp.eye(ROWS, dtype=jnp.float32)
    image_dir = jnp.zeros((N_GRP, N_BLK, ROWS, D), jnp.float32)
    text_dir = jnp.zeros((N_GRP, N_BLK, ROWS, D), jnp.float32)
    for group_step, block_step in ((0, 0), (0, 1), (0, 2), (1, 0)):
        paired_block = jnp.roll(text_lower_half, (group_step, block_step), axis=(0, 1)).astype(jnp.float32)
        pair_scores = scale_factor * jnp.einsum('qcox,qcux->qcou', image_full_width, paired_block) + block_distance
        if group_step == 0 and block_step == 0:
            target_sign = 2.0 * identity - 1.0
        else:
            target_sign = -jnp.ones_like(identity)
        pair_weight_factor = (scale_factor * -target_sign * jax.nn.sigmoid(-target_sign * pair_scores)).astype(jnp.bfloat16)
        pair_weight_factor = pair_weight_factor.astype(jnp.float32)
        image_dir = image_dir + jnp.einsum('gbrs,gbsd->gbrd', pair_weight_factor, paired_block)
        terms = jnp.einsum('gbrs,gbrd->gbsd', pair_weight_factor, image_full_width)
        text_dir = text_dir + jnp.roll(terms, (-group_step, -block_step), axis=(0, 1))
    image_dir = image_dir.reshape(BATCH, D)
    text_dir = text_dir.reshape(BATCH, D)
    image_grad = (image_dir - image_unit * lax.optimization_barrier(jnp.sum(image_unit * image_dir, axis=-1, keepdims=True))) / image_norm
    text_grad = (text_dir - text_unit * lax.optimization_barrier(jnp.sum(text_unit * text_dir, axis=-1, keepdims=True))) / text_norm
    return (image_grad, text_grad)
```

```python
import functools

import jax
import jax.numpy as jnp
from jax import lax
from jax.experimental import pallas as pl
from jax.experimental.pallas import tpu as pltpu
from jax.sharding import PartitionSpec as P

EPSILON = 1e-06
D = 1152
ROWS = 1024
HALF = 512
TILE = 256
AXES = ("grp", "blk")
WIDE = 384
VMEM_LIMIT = 50 * 1024 * 1024
COST = pl.CostEstimate(flops=0, bytes_accessed=0, transcendentals=0)


def device(z, y, x, c):
    return (((z % 4) * 4 + y % 4) * 4 + x % 4) * 2 + c


def route(target):
    pairs = []
    for z in range(4):
        for y in range(4):
            for x in range(4):
                for c in range(2):
                    pairs.append((device(z, y, x, c), device(*target(z, y, x, c))))
    return pairs


def inner_first(is_text, x):
    return (x >= 2) == is_text


def first_hop(is_text):
    def target(z, y, x, c):
        return (z, y ^ 1 if inner_first(is_text(c), x) else 3 - y, x, c)

    return target


def second_hop(is_text):
    def target(z, y, x, c):
        inner = inner_first(is_text(c), x)
        origin = y ^ 1 if inner else 3 - y
        to = 3 - y if inner else y ^ 1
        if is_text(c):
            z += 1 if origin >= 2 else 0
        else:
            z -= 1 if origin < 2 else 0
        return (z, to, x, c)

    return target


def along(is_text):
    return lambda z, y, x, c: (z, y, x + 1 if is_text(c) else x - 1, c)


def other_core(z, y, x, c):
    return (z, y, x, 1 - c)


def a_is_text(c):
    return c == 1


def b_is_text(c):
    return c == 0


def send(name, value, target):
    with jax.named_scope(name):
        return lax.ppermute(value, AXES, route(target))


def after(values, *others):
    held = lax.optimization_barrier((tuple(values), tuple(others)))
    return held[0]


def normalized(raw):
    values = raw.astype(jnp.float32)
    inverse = 1.0 / jnp.sqrt(jnp.sum(values * values, axis=-1, keepdims=True) + EPSILON)
    return values * inverse, inverse


def all_rows_kernel(core, images, texts, a, b, a_0, b_0, a_1, b_1, image_inverse, text_inverse):
    image_unit, inverse = normalized(images[...])
    image_unit = image_unit.astype(jnp.bfloat16)
    image_inverse[...] = inverse
    text_unit, inverse = normalized(texts[...])
    text_unit = text_unit.astype(jnp.bfloat16)
    text_inverse[...] = inverse
    a_value = jnp.where(core[0] == 0, image_unit, text_unit)
    b_value = jnp.where(core[0] == 0, text_unit, image_unit)
    a[...] = a_value
    b[...] = b_value
    a_1[...] = a_value
    b_1[...] = b_value

    @pl.when(pl.program_id(0) == 0)
    def _():
        a_0[...] = a_value
        b_0[...] = b_value


def all_rows(core, images, texts):
    spec = pl.BlockSpec((HALF, D), lambda i: (i, 0))
    part_spec = pl.BlockSpec((HALF, D), lambda i: (0, 0))
    column = pl.BlockSpec((HALF, 1), lambda i: (i, 0))
    whole = jax.ShapeDtypeStruct((ROWS, D), jnp.bfloat16)
    part = jax.ShapeDtypeStruct((HALF, D), jnp.bfloat16)
    scale = jax.ShapeDtypeStruct((ROWS, 1), jnp.float32)
    return pl.pallas_call(
        all_rows_kernel,
        grid=(2,),
        in_specs=[pl.BlockSpec(memory_space=pltpu.SMEM), spec, spec],
        out_specs=[spec, spec] + [part_spec] * 4 + [column, column],
        out_shape=[whole, whole] + [part] * 4 + [scale, scale],
        compiler_params=pltpu.CompilerParams(vmem_limit_bytes=VMEM_LIMIT),
        cost_estimate=COST,
    )(core, images, texts)


def coefficients(dots, scalars, diagonal_at=None):
    bent = jnp.tanh(dots * scalars[0] + scalars[1])
    if diagonal_at is None:
        return ((bent + 1.0) * scalars[0]).astype(jnp.bfloat16)
    down = lax.broadcasted_iota(jnp.int32, dots.shape, 0)
    across = lax.broadcasted_iota(jnp.int32, dots.shape, 1) + diagonal_at
    return ((bent + jnp.where(across == down, -1.0, 1.0)) * scalars[0]).astype(jnp.bfloat16)


def row_dots(own, paired):
    return lax.dot_general(own, paired, (((1,), (1,)), ((), ())), preferred_element_type=jnp.float32)


def pairs_kernel(count, has_own, has_before, scalars, own, *refs):
    partners = refs[:count]
    total, factors = refs[count + has_before : count + has_before + 2]
    step = pl.program_id(0)

    def columns(part):
        return slice(part * WIDE, (part + 1) * WIDE)

    if has_before:
        before = refs[count]
        held, arrived = refs[-2:]
        loads = [
            pltpu.make_async_copy(before.at[:, columns(part)], held.at[:, columns(part)], arrived.at[part])
            for part in range(D // WIDE)
        ]

        @pl.when(step == 0)
        def _():
            for load in loads:
                load.start()

    base = 0
    for at, partner in enumerate(partners):
        def make(at=at, partner=partner, base=base):
            for start in range(0, partner.shape[0], TILE):
                dots = row_dots(own[...], partner[start : start + TILE, :])
                diagonal_at = start if has_own and at == 0 else None
                factors[:, base + start : base + start + TILE] = coefficients(dots, scalars, diagonal_at)

        pl.when(step == at)(make)
        base += partner.shape[0]

    for part in range(D // WIDE):
        def add(part=part):
            result = None
            if has_before:
                loads[part].wait()
                result = held[:, columns(part)]
            base = 0
            for partner in partners:
                rows = partner.shape[0]
                term = jnp.dot(factors[:, base : base + rows], partner[:, columns(part)], preferred_element_type=jnp.float32)
                result = term if result is None else result + term
                base += rows
            total[...] = result

        pl.when(step == count + part)(add)


def pairs(scalars, own, partners, before=None, has_own=False):
    count = len(partners)
    rows = sum(partner.shape[0] for partner in partners)
    once = pl.Buffered(1)
    has_before = before is not None
    return pl.pallas_call(
        functools.partial(pairs_kernel, count, has_own, int(has_before)),
        grid=(count + D // WIDE,),
        in_specs=[
            pl.BlockSpec(memory_space=pltpu.SMEM),
            pl.BlockSpec((ROWS, D), lambda i: (0, 0), pipeline_mode=once),
            *[pl.BlockSpec(partner.shape, lambda i: (0, 0), pipeline_mode=once) for partner in partners],
            *([pl.BlockSpec(memory_space=pl.ANY)] if has_before else []),
        ],
        out_specs=pl.BlockSpec((ROWS, WIDE), lambda i: (0, jnp.maximum(i - count, 0))),
        out_shape=jax.ShapeDtypeStruct((ROWS, D), jnp.float32),
        scratch_shapes=[
            pltpu.VMEM((ROWS, rows), jnp.bfloat16),
            *([pltpu.VMEM((ROWS, D), jnp.float32), pltpu.SemaphoreType.DMA((D // WIDE,))] if has_before else []),
        ],
        compiler_params=pltpu.CompilerParams(vmem_limit_bytes=VMEM_LIMIT),
        cost_estimate=COST,
    )(scalars, own, *partners, *([before] if has_before else []))


def last_kernel(core, scalars, a_pair, b_pair, images, texts, image_inverse, text_inverse, a_before, b_before, image_grad, text_grad):
    is_zero = core[0] == 0
    image_unit = images[...].astype(jnp.float32) * image_inverse[...]
    text_unit = texts[...].astype(jnp.float32) * text_inverse[...]
    grads = []
    for unit, scale, paired, before in (
        (jnp.where(is_zero, image_unit, text_unit), jnp.where(is_zero, image_inverse[...], text_inverse[...]), a_pair, a_before),
        (jnp.where(is_zero, text_unit, image_unit), jnp.where(is_zero, text_inverse[...], image_inverse[...]), b_pair, b_before),
    ):
        own = unit.astype(jnp.bfloat16)
        total = before[...]
        for start in range(0, paired.shape[0], TILE):
            rows = paired[start : start + TILE, :]
            factor = coefficients(row_dots(own, rows), scalars)
            total = total + jnp.dot(factor, rows, preferred_element_type=jnp.float32)
        inside = jnp.sum(unit * total, axis=-1, keepdims=True)
        grads.append((total - unit * inside) * scale)
    image_grad[...] = jnp.where(is_zero, grads[0], grads[1])
    text_grad[...] = jnp.where(is_zero, grads[1], grads[0])


def last_pairs(core, scalars, a_pair, b_pair, images, texts, image_inverse, text_inverse, a_before, b_before):
    rows = a_pair.shape[0]
    spec = pl.BlockSpec((TILE, D), lambda i: (i, 0))
    column = pl.BlockSpec((TILE, 1), lambda i: (i, 0))
    pair = pl.BlockSpec((rows, D), lambda i: (0, 0))
    grad = jax.ShapeDtypeStruct((ROWS, D), jnp.float32)
    scalar = pl.BlockSpec(memory_space=pltpu.SMEM)
    return pl.pallas_call(
        last_kernel,
        grid=(ROWS // TILE,),
        in_specs=[scalar, scalar, pair, pair, spec, spec, column, column, spec, spec],
        out_specs=[spec, spec],
        out_shape=[grad, grad],
        compiler_params=pltpu.CompilerParams(vmem_limit_bytes=VMEM_LIMIT),
        cost_estimate=COST,
    )(core, scalars, a_pair, b_pair, images, texts, image_inverse, text_inverse, a_before, b_before)


def body(images, texts, log_logit_scale, bias):
    scalars = 0.5 * jnp.concatenate([jnp.exp(log_logit_scale), bias])
    index = lax.axis_index(AXES).astype(jnp.int32)
    core = lax.rem(index, 2)
    x = lax.rem(lax.div(index, 2), 4)
    which = jnp.reshape(core, (1,))
    text_end, image_end = x == 3, x == 0
    a_end = jnp.where(core == 0, image_end, text_end)
    b_end = jnp.where(core == 0, text_end, image_end)

    a, b, a_0, b_0, a_1, b_1, image_inverse, text_inverse = all_rows(which, images, texts)
    a_01 = send("a_01", a_0, first_hop(a_is_text))
    b_01 = send("b_01", b_0, first_hop(b_is_text))
    near = send("near", b, other_core)
    a_sum = pairs(scalars, a, [b], has_own=True)
    b_sum = pairs(scalars, b, [a, near], has_own=True)

    a_1, b_1, a_sum, b_sum = after((a_1, b_1, a_sum, b_sum))
    a_11 = send("a_11", a_1, first_hop(a_is_text))
    b_11 = send("b_11", b_1, first_hop(b_is_text))
    a_01, b_01, b_sum = after((a_01, b_01, b_sum))
    a_x0 = send("a_x0", jnp.where(a_end, a_01, a_0), along(a_is_text))
    b_x0 = send("b_x0", jnp.where(b_end, b_01, b_0), along(b_is_text))

    a_01, b_01 = after((a_01, b_01), a_11, b_11)
    a_02 = send("a_02", a_01, second_hop(a_is_text))
    b_02 = send("b_02", b_01, second_hop(b_is_text))
    a_x1 = send("a_x1", jnp.where(a_end, a_11, a_1), along(a_is_text))
    b_x1 = send("b_x1", jnp.where(b_end, b_11, b_1), along(b_is_text))
    far_0 = send("far_0", a_x0, other_core)
    b_sum = pairs(scalars, b, [a_x0], b_sum)
    a_sum = pairs(scalars, a, [b_x0, far_0], a_sum)

    a_11, b_11, a_sum, b_sum = after((a_11, b_11, a_sum, b_sum), a_02, b_02)
    a_12 = send("a_12", a_11, second_hop(a_is_text))
    b_12 = send("b_12", b_11, second_hop(b_is_text))
    far_1 = send("far_1", a_x1, other_core)
    b_sum = pairs(scalars, b, [a_02, a_x1], b_sum)
    a_sum = pairs(scalars, a, [b_02, b_x1, far_1], a_sum)

    return tuple(
        last_pairs(which, scalars, b_12, a_12, images, texts, image_inverse, text_inverse, a_sum, b_sum)
    )


def solution(mesh):
    return jax.shard_map(
        body,
        mesh=mesh,
        in_specs=(P(AXES, None), P(AXES, None), P(), P()),
        out_specs=(P(AXES, None), P(AXES, None)),
        check_vma=False,
    )
```

```python
import functools

import jax
import jax.numpy as jnp
from jax import lax
from jax.experimental import pallas as pl
from jax.experimental.pallas import tpu as pltpu
from jax.sharding import PartitionSpec as P

EPSILON = 1e-06
D = 1152
ROWS = 1024
HALF = 512
TILE = 256
AXES = ("grp", "blk")
WIDE = 384
FEW = 32
VMEM_LIMIT = 46 * 1024 * 1024
EDGE_LIMIT = 63 * 1024 * 1024
COST = pl.CostEstimate(flops=0, bytes_accessed=0, transcendentals=0)


def device(z, y, x, c):
    return (((z % 4) * 4 + y % 4) * 4 + x % 4) * 2 + c


def route(target):
    pairs = []
    for z in range(4):
        for y in range(4):
            for x in range(4):
                for c in range(2):
                    pairs.append((device(z, y, x, c), device(*target(z, y, x, c))))
    return pairs


def inner_first(is_text, x):
    return (x >= 2) == is_text


def first_hop(is_text):
    def target(z, y, x, c):
        return (z, y ^ 1 if inner_first(is_text(c), x) else 3 - y, x, c)

    return target


def second_hop(is_text):
    def target(z, y, x, c):
        inner = inner_first(is_text(c), x)
        origin = y ^ 1 if inner else 3 - y
        to = 3 - y if inner else y ^ 1
        if is_text(c):
            z += 1 if origin >= 2 else 0
        else:
            z -= 1 if origin < 2 else 0
        return (z, to, x, c)

    return target


def along(is_text):
    return lambda z, y, x, c: (z, y, x + 1 if is_text(c) else x - 1, c)


def other_core(z, y, x, c):
    return (z, y, x, 1 - c)


def a_is_text(c):
    return c == 1


def b_is_text(c):
    return c == 0


def send(name, value, target):
    with jax.named_scope(name):
        return lax.ppermute(value, AXES, route(target))


def after(values, *others):
    held = lax.optimization_barrier((tuple(values), tuple(others)))
    return held[0]


def scale_of(squares):
    return 1.0 / jnp.sqrt(squares + EPSILON)


def pieces(rows):
    return [slice(start, start + FEW) for start in range(0, rows, FEW)]


def normalized(raw):
    values = raw.astype(jnp.float32)
    scale = scale_of(jnp.sum(values * values, axis=-1, keepdims=True))
    return values * scale, scale


def half_kernel(core, images, texts, a, b):
    for rows in pieces(TILE):
        image_unit = normalized(images[rows, :])[0]
        text_unit = normalized(texts[rows, :])[0]
        a[rows, :] = jnp.where(core[0] == 0, image_unit, text_unit).astype(jnp.bfloat16)
        b[rows, :] = jnp.where(core[0] == 0, text_unit, image_unit).astype(jnp.bfloat16)


def half(core, images, texts, first):
    spec = pl.BlockSpec((TILE, D), lambda i: (i + first // TILE, 0))
    out = pl.BlockSpec((TILE, D), lambda i: (i, 0))
    shape = jax.ShapeDtypeStruct((HALF, D), jnp.bfloat16)
    return pl.pallas_call(
        half_kernel,
        grid=(HALF // TILE,),
        in_specs=[pl.BlockSpec(memory_space=pltpu.SMEM), spec, spec],
        out_specs=[out, out],
        out_shape=[shape, shape],
        compiler_params=pltpu.CompilerParams(vmem_limit_bytes=EDGE_LIMIT),
        cost_estimate=COST,
    )(core, images, texts)


def coefficients(dots, scalars, diagonal_at=None):
    bent = jnp.tanh(dots * scalars[0] + scalars[1])
    if diagonal_at is None:
        return ((bent + 1.0) * scalars[0]).astype(jnp.bfloat16)
    down = lax.broadcasted_iota(jnp.int32, dots.shape, 0)
    across = lax.broadcasted_iota(jnp.int32, dots.shape, 1) + diagonal_at
    return ((bent + jnp.where(across == down, -1.0, 1.0)) * scalars[0]).astype(jnp.bfloat16)


def row_dots(own, paired):
    return lax.dot_general(own, paired, (((1,), (1,)), ((), ())), preferred_element_type=jnp.float32)


class Side:
    def __init__(self, owns, partners, before=None, has_own=False):
        self.owns, self.partners, self.before, self.has_own = owns, partners, before, has_own
        self.count = len(partners)
        self.rows = sum(partner.shape[0] for partner in partners)
        self.steps = self.count + D // WIDE


def columns(part):
    return slice(part * WIDE, (part + 1) * WIDE)


def side_steps(side, first, scalars, owns, partners, before, held, arrived, total, factors):
    step = pl.program_id(0)
    loads = []
    if before is not None:
        loads = [
            pltpu.make_async_copy(before.at[:, columns(part)], held.at[:, columns(part)], arrived.at[part])
            for part in range(D // WIDE)
        ]

        @pl.when(step == 0)
        def _():
            for load in loads:
                load.start()

    base = 0
    for at, partner in enumerate(partners):
        def make(partner=partner, base=base):
            for start in range(0, partner.shape[0], TILE):
                for half_at, own in enumerate(owns):
                    top = half_at * HALF
                    dots = row_dots(own[...], partner[start : start + TILE, :])
                    diagonal_at = base + start - top if side.has_own and base < ROWS else None
                    factors[top : top + own.shape[0], base + start : base + start + TILE] = coefficients(
                        dots, scalars, diagonal_at
                    )

        pl.when(step == first + at)(make)
        base += partner.shape[0]

    for part in range(D // WIDE):
        def add(part=part):
            result = None
            if loads:
                loads[part].wait()
                result = held[:, columns(part)]
            base = 0
            for partner in partners:
                rows = partner.shape[0]
                term = jnp.dot(factors[:, base : base + rows], partner[:, columns(part)], preferred_element_type=jnp.float32)
                result = term if result is None else result + term
                base += rows
            total[...] = result

        pl.when(step == first + side.count + part)(add)


def pairs_kernel(sides, scalars, *refs):
    refs = list(refs)
    take = lambda count: [refs.pop(0) for _ in range(count)]
    inputs = [(take(2), take(side.count), take(1)[0] if side.before is not None else None) for side in sides]
    totals = take(len(sides))
    factors = take(1)[0]
    first = 0
    for side, (owns, partners, before), total in zip(sides, inputs, totals):
        held, arrived = take(2) if before is not None else (None, None)
        side_steps(side, first, scalars, owns, partners, before, held, arrived, total, factors)
        first += side.steps


def pairs(scalars, *sides):
    specs, values, out_specs, scratch = [], [], [], []
    first = 0
    for side in sides:
        for value in (*side.owns, *side.partners):
            specs.append(pl.BlockSpec(value.shape, lambda i: (0, 0), pipeline_mode=pl.Buffered(1)))
            values.append(value)
        if side.before is not None:
            specs.append(pl.BlockSpec(memory_space=pl.ANY))
            values.append(side.before)
            scratch += [pltpu.VMEM((ROWS, D), jnp.float32), pltpu.SemaphoreType.DMA((D // WIDE,))]
        begin = first + side.count
        last = D // WIDE - 1
        out_specs.append(pl.BlockSpec((ROWS, WIDE), lambda i, begin=begin: (0, jnp.clip(i - begin, 0, last))))
        first += side.steps
    factors = pltpu.VMEM((ROWS, max(side.rows for side in sides)), jnp.bfloat16)
    return pl.pallas_call(
        functools.partial(pairs_kernel, sides),
        grid=(first,),
        in_specs=[pl.BlockSpec(memory_space=pltpu.SMEM), *specs],
        out_specs=out_specs,
        out_shape=[jax.ShapeDtypeStruct((ROWS, D), jnp.float32)] * len(sides),
        scratch_shapes=[factors, *scratch],
        compiler_params=pltpu.CompilerParams(vmem_limit_bytes=VMEM_LIMIT),
        cost_estimate=COST,
    )(scalars, *values)


def last_kernel(core, scalars, a_pair, b_pair, images, texts, a_before, b_before, image_grad, text_grad, pair, before, arrived):
    step = pl.program_id(0)
    count = ROWS // TILE

    def rows_at(at):
        return pl.ds(pl.multiple_of(at * TILE, TILE), TILE)

    def copies(pair_sources, before_sources):
        found = []
        for side in range(2):
            found.append(pltpu.make_async_copy(pair_sources[side], pair.at[side], arrived.at[side, count]))
        for at in range(count):
            for side in range(2):
                rows = pl.ds(at * TILE, TILE)
                found.append(pltpu.make_async_copy(before_sources[side].at[rows], before.at[side, rows], arrived.at[side, at]))
        return found

    @pl.when(jnp.logical_and(step == 0, core[0] == 0))
    def _():
        for copy in copies((a_pair, b_pair), (a_before, b_before)):
            copy.start()

    @pl.when(jnp.logical_and(step == 0, core[0] != 0))
    def _():
        for copy in copies((b_pair, a_pair), (b_before, a_before)):
            copy.start()

    @pl.when(step == 0)
    def _():
        for side in range(2):
            pltpu.make_async_copy(a_pair, pair.at[side], arrived.at[side, count]).wait()

    rows = rows_at(step)
    for side, (raw, grad) in enumerate(((images, image_grad), (texts, text_grad))):
        unit, scale = normalized(raw[...])
        own = unit.astype(jnp.bfloat16)
        total = None
        for start in range(0, a_pair.shape[0], TILE):
            values = pair[side, start : start + TILE, :]
            factor = coefficients(row_dots(own, values), scalars)
            term = jnp.dot(factor, values, preferred_element_type=jnp.float32)
            total = term if total is None else total + term
        pltpu.make_async_copy(a_before.at[rows], before.at[side, rows], arrived.at[side, step]).wait()
        total = total + before[side, rows, :]
        inside = jnp.sum(unit * total, axis=-1, keepdims=True)
        grad[...] = (total - unit * inside) * scale


def last_pairs(core, scalars, a_pair, b_pair, images, texts, a_before, b_before):
    spec = pl.BlockSpec((TILE, D), lambda i: (i, 0))
    grad = jax.ShapeDtypeStruct((ROWS, D), jnp.float32)
    scalar = pl.BlockSpec(memory_space=pltpu.SMEM)
    anywhere = pl.BlockSpec(memory_space=pl.ANY)
    return pl.pallas_call(
        last_kernel,
        grid=(ROWS // TILE,),
        in_specs=[scalar, scalar, anywhere, anywhere, spec, spec, anywhere, anywhere],
        out_specs=[spec, spec],
        out_shape=[grad, grad],
        scratch_shapes=[
            pltpu.VMEM((2, *a_pair.shape), jnp.bfloat16),
            pltpu.VMEM((2, ROWS, D), jnp.float32),
            pltpu.SemaphoreType.DMA((2, ROWS // TILE + 1)),
        ],
        compiler_params=pltpu.CompilerParams(vmem_limit_bytes=EDGE_LIMIT),
        cost_estimate=COST,
    )(core, scalars, a_pair, b_pair, images, texts, a_before, b_before)


def body(images, texts, log_logit_scale, bias):
    scalars = 0.5 * jnp.concatenate([jnp.exp(log_logit_scale), bias])
    index = lax.axis_index(AXES).astype(jnp.int32)
    core = lax.rem(index, 2)
    x = lax.rem(lax.div(index, 2), 4)
    which = jnp.reshape(core, (1,))
    text_end, image_end = x == 3, x == 0
    a_end = jnp.where(core == 0, image_end, text_end)
    b_end = jnp.where(core == 0, text_end, image_end)

    a_0, b_0 = half(which, images, texts, 0)
    a_01 = send("a_01", a_0, first_hop(a_is_text))
    b_01 = send("b_01", b_0, first_hop(b_is_text))
    near_0 = send("near_0", b_0, other_core)
    rest = after((images, texts), a_0, b_0)
    a_1, b_1 = half(which, *rest, HALF)
    a, b = (a_0, a_1), (b_0, b_1)
    a_sum, = pairs(scalars, Side(a, b, has_own=True))
    b_near, = after((b_1,), a_sum)
    near_1 = send("near_1", b_near, other_core)

    a_1, b_1, a_sum = after((a_1, b_1, a_sum), near_0)
    a_11 = send("a_11", a_1, first_hop(a_is_text))
    b_11 = send("b_11", b_1, first_hop(b_is_text))
    a_01, b_01, a_sum = after((a_01, b_01, a_sum))
    a_x0 = send("a_x0", jnp.where(a_end, a_01, a_0), along(a_is_text))
    b_x0 = send("b_x0", jnp.where(b_end, b_01, b_0), along(b_is_text))
    near_0, near_1, a_sum = after((near_0, near_1, a_sum), a_01, b_01)
    b_sum, = pairs(scalars, Side(b, [*a, near_0, near_1], has_own=True))

    a_01, b_01, b_sum = after((a_01, b_01, b_sum), a_11, b_11)
    a_02 = send("a_02", a_01, second_hop(a_is_text))
    b_02 = send("b_02", b_01, second_hop(b_is_text))
    a_x1 = send("a_x1", jnp.where(a_end, a_11, a_1), along(a_is_text))
    b_x1 = send("b_x1", jnp.where(b_end, b_11, b_1), along(b_is_text))
    far_0 = send("far_0", a_x0, other_core)
    b_sum, a_sum = pairs(scalars, Side(b, [a_x0], b_sum), Side(a, [b_x0, far_0], a_sum))

    a_11, b_11, a_sum, b_sum = after((a_11, b_11, a_sum, b_sum), a_02, b_02)
    a_12 = send("a_12", a_11, second_hop(a_is_text))
    b_12 = send("b_12", b_11, second_hop(b_is_text))
    a_x1, a_sum = after((a_x1, a_sum))
    far_1 = send("far_1", a_x1, other_core)
    b_sum, a_sum = pairs(scalars, Side(b, [a_02, a_x1], b_sum), Side(a, [b_02, b_x1, far_1], a_sum))

    return tuple(last_pairs(which, scalars, b_12, a_12, images, texts, a_sum, b_sum))


def solution(mesh):
    return jax.shard_map(
        body,
        mesh=mesh,
        in_specs=(P(AXES, None), P(AXES, None), P(), P()),
        out_specs=(P(AXES, None), P(AXES, None)),
        check_vma=False,
    )
```

```python
import functools

import jax
import jax.numpy as jnp
from jax import lax
from jax.experimental import pallas as pl
from jax.experimental.pallas import tpu as pltpu
from jax.sharding import PartitionSpec as P

EPSILON = 1e-06
D = 1152
ROWS = 1024
HALF = 512
TILE = 256
AXES = ("grp", "blk")
WIDE = 384
FEW = 32
VMEM_LIMIT = 48 * 1024 * 1024
EDGE_LIMIT = 63 * 1024 * 1024
COST = pl.CostEstimate(flops=0, bytes_accessed=0, transcendentals=0)


def device(z, y, x, c):
    return (((z % 4) * 4 + y % 4) * 4 + x % 4) * 2 + c


def route(target):
    pairs = []
    for z in range(4):
        for y in range(4):
            for x in range(4):
                for c in range(2):
                    pairs.append((device(z, y, x, c), device(*target(z, y, x, c))))
    return pairs


def inner_first(is_text, x):
    return (x >= 2) == is_text


def first_hop(is_text):
    def target(z, y, x, c):
        return (z, y ^ 1 if inner_first(is_text(c), x) else 3 - y, x, c)

    return target


def second_hop(is_text):
    def target(z, y, x, c):
        inner = inner_first(is_text(c), x)
        origin = y ^ 1 if inner else 3 - y
        to = 3 - y if inner else y ^ 1
        if is_text(c):
            z += 1 if origin >= 2 else 0
        else:
            z -= 1 if origin < 2 else 0
        return (z, to, x, c)

    return target


def along(is_text):
    return lambda z, y, x, c: (z, y, x + 1 if is_text(c) else x - 1, c)


def other_core(z, y, x, c):
    return (z, y, x, 1 - c)


def a_is_text(c):
    return c == 1


def b_is_text(c):
    return c == 0


def send(name, value, target):
    with jax.named_scope(name):
        return lax.ppermute(value, AXES, route(target))


def after(values, *others):
    held = lax.optimization_barrier((tuple(values), tuple(others)))
    return held[0]


def scale_of(squares):
    return 1.0 / jnp.sqrt(squares + EPSILON)


def pieces(rows):
    return [slice(start, start + FEW) for start in range(0, rows, FEW)]


def normalized(raw):
    values = raw.astype(jnp.float32)
    scale = scale_of(jnp.sum(values * values, axis=-1, keepdims=True))
    return values * scale, scale


def half_kernel(core, images, texts, a, b):
    for rows in pieces(TILE):
        image_unit = normalized(images[rows, :])[0]
        text_unit = normalized(texts[rows, :])[0]
        a[rows, :] = jnp.where(core[0] == 0, image_unit, text_unit).astype(jnp.bfloat16)
        b[rows, :] = jnp.where(core[0] == 0, text_unit, image_unit).astype(jnp.bfloat16)


def half(core, images, texts, first):
    spec = pl.BlockSpec((TILE, D), lambda i: (i + first // TILE, 0))
    out = pl.BlockSpec((TILE, D), lambda i: (i, 0))
    shape = jax.ShapeDtypeStruct((HALF, D), jnp.bfloat16)
    return pl.pallas_call(
        half_kernel,
        grid=(HALF // TILE,),
        in_specs=[pl.BlockSpec(memory_space=pltpu.SMEM), spec, spec],
        out_specs=[out, out],
        out_shape=[shape, shape],
        compiler_params=pltpu.CompilerParams(vmem_limit_bytes=EDGE_LIMIT),
        cost_estimate=COST,
    )(core, images, texts)


def coefficients(dots, scalars, diagonal_at=None):
    bent = jnp.tanh(dots * scalars[0] + scalars[1])
    if diagonal_at is None:
        return ((bent + 1.0) * scalars[0]).astype(jnp.bfloat16)
    down = lax.broadcasted_iota(jnp.int32, dots.shape, 0)
    across = lax.broadcasted_iota(jnp.int32, dots.shape, 1) + diagonal_at
    return ((bent + jnp.where(across == down, -1.0, 1.0)) * scalars[0]).astype(jnp.bfloat16)


def row_dots(own, paired):
    return lax.dot_general(own, paired, (((1,), (1,)), ((), ())), preferred_element_type=jnp.float32)


class Side:
    def __init__(self, owns, partners, before=None, has_own=False):
        self.owns, self.partners, self.before, self.has_own = owns, partners, before, has_own
        self.count = len(partners)
        self.rows = sum(partner.shape[0] for partner in partners)
        self.steps = self.count + D // WIDE


def columns(part):
    return slice(part * WIDE, (part + 1) * WIDE)


def side_steps(side, first, scalars, owns, partners, before, held, arrived, total, factors):
    step = pl.program_id(0)
    loads = []
    if before is not None:
        loads = [
            pltpu.make_async_copy(before.at[:, columns(part)], held.at[:, columns(part)], arrived.at[part])
            for part in range(D // WIDE)
        ]

        @pl.when(step == 0)
        def _():
            for load in loads:
                load.start()

    base = 0
    for at, partner in enumerate(partners):
        def make(partner=partner, base=base):
            for start in range(0, partner.shape[0], TILE):
                for half_at, own in enumerate(owns):
                    top = half_at * HALF
                    dots = row_dots(own[...], partner[start : start + TILE, :])
                    diagonal_at = base + start - top if side.has_own and base < ROWS else None
                    factors[top : top + own.shape[0], base + start : base + start + TILE] = coefficients(
                        dots, scalars, diagonal_at
                    )

        pl.when(step == first + at)(make)
        base += partner.shape[0]

    for part in range(D // WIDE):
        def add(part=part):
            result = None
            if loads:
                loads[part].wait()
                result = held[:, columns(part)]
            base = 0
            for partner in partners:
                rows = partner.shape[0]
                term = jnp.dot(factors[:, base : base + rows], partner[:, columns(part)], preferred_element_type=jnp.float32)
                result = term if result is None else result + term
                base += rows
            total[...] = result

        pl.when(step == first + side.count + part)(add)


def pairs_kernel(sides, has_stack, scalars, *refs):
    refs = list(refs)
    take = lambda count: [refs.pop(0) for _ in range(count)]
    inputs = [(take(2), take(side.count), take(1)[0] if side.before is not None else None) for side in sides]
    take(has_stack)
    totals = take(len(sides))
    factors = take(1)[0]
    first = 0
    for side, (owns, partners, before), total in zip(sides, inputs, totals):
        held, arrived = take(2) if before is not None else (None, None)
        side_steps(side, first, scalars, owns, partners, before, held, arrived, total, factors)
        first += side.steps


def pairs(scalars, *sides, at=None, stack=None):
    specs, values, out_specs, scratch = [], [], [], []
    first = 0
    for side in sides:
        for value in (*side.owns, *side.partners):
            specs.append(pl.BlockSpec(value.shape, lambda i: (0, 0), pipeline_mode=pl.Buffered(1)))
            values.append(value)
        if side.before is not None:
            specs.append(pl.BlockSpec(memory_space=pl.ANY))
            values.append(side.before)
            scratch += [pltpu.VMEM((ROWS, D), jnp.float32), pltpu.SemaphoreType.DMA((D // WIDE,))]
        begin = first + side.count
        last = D // WIDE - 1
        out_specs.append(pl.BlockSpec((ROWS, WIDE), lambda i, begin=begin: (0, jnp.clip(i - begin, 0, last))))
        first += side.steps
    factors = pltpu.VMEM((ROWS, max(side.rows for side in sides)), jnp.bfloat16)
    shape = jax.ShapeDtypeStruct((ROWS, D), jnp.float32)
    if at is not None:
        shape = jax.ShapeDtypeStruct((2, ROWS, D), jnp.float32)
        out_specs = [pl.BlockSpec((None, ROWS, WIDE), lambda i: (at, 0, jnp.clip(i - sides[0].count, 0, D // WIDE - 1)))]
    aliases = {}
    if stack is not None:
        specs.append(pl.BlockSpec(memory_space=pl.ANY))
        values.append(stack)
        aliases = {len(values): 0}
    return pl.pallas_call(
        functools.partial(pairs_kernel, sides, int(stack is not None)),
        grid=(first,),
        in_specs=[pl.BlockSpec(memory_space=pltpu.SMEM), *specs],
        out_specs=out_specs,
        out_shape=[shape] * len(sides),
        input_output_aliases=aliases,
        scratch_shapes=[factors, *scratch],
        compiler_params=pltpu.CompilerParams(vmem_limit_bytes=VMEM_LIMIT),
        cost_estimate=COST,
    )(scalars, *values)


def last_kernel(core, scalars, a_pair, b_pair, images, texts, image_before, text_before, image_grad, text_grad, pair):
    @pl.when(pl.program_id(0) == 0)
    def _():
        is_zero = core[0] == 0
        pair[0] = jnp.where(is_zero, a_pair[...], b_pair[...])
        pair[1] = jnp.where(is_zero, b_pair[...], a_pair[...])

    for side, (raw, before, grad) in enumerate(((images, image_before, image_grad), (texts, text_before, text_grad))):
        unit, scale = normalized(raw[...])
        own = unit.astype(jnp.bfloat16)
        factor = jnp.concatenate(
            [
                coefficients(row_dots(own, pair[side, start : start + TILE, :]), scalars)
                for start in range(0, a_pair.shape[0], TILE)
            ],
            axis=1,
        )
        total = before[...] + jnp.dot(factor, pair[side], preferred_element_type=jnp.float32)
        inside = jnp.sum(unit * total, axis=-1, keepdims=True)
        grad[...] = (total - unit * inside) * scale


def last_pairs(core, scalars, a_pair, b_pair, images, texts, before):
    spec = pl.BlockSpec((TILE, D), lambda i, core: (i, 0))
    image_before = pl.BlockSpec((None, TILE, D), lambda i, core: (core[0], i, 0))
    text_before = pl.BlockSpec((None, TILE, D), lambda i, core: (1 - core[0], i, 0))
    whole = pl.BlockSpec(a_pair.shape, lambda i, core: (0, 0), pipeline_mode=pl.Buffered(1))
    grad = jax.ShapeDtypeStruct((ROWS, D), jnp.float32)
    return pl.pallas_call(
        last_kernel,
        grid_spec=pltpu.PrefetchScalarGridSpec(
            num_scalar_prefetch=1,
            grid=(ROWS // TILE,),
            in_specs=[
                pl.BlockSpec(memory_space=pltpu.SMEM), whole, whole, spec, spec, image_before, text_before,
            ],
            out_specs=[spec, spec],
            scratch_shapes=[pltpu.VMEM((2, *a_pair.shape), jnp.bfloat16)],
        ),
        out_shape=[grad, grad],
        compiler_params=pltpu.CompilerParams(vmem_limit_bytes=EDGE_LIMIT),
        cost_estimate=COST,
    )(core, scalars, a_pair, b_pair, images, texts, before, before)


def body(images, texts, log_logit_scale, bias):
    scalars = 0.5 * jnp.concatenate([jnp.exp(log_logit_scale), bias])
    index = lax.axis_index(AXES).astype(jnp.int32)
    core = lax.rem(index, 2)
    x = lax.rem(lax.div(index, 2), 4)
    which = jnp.reshape(core, (1,))
    text_end, image_end = x == 3, x == 0
    a_end = jnp.where(core == 0, image_end, text_end)
    b_end = jnp.where(core == 0, text_end, image_end)

    a_0, b_0 = half(which, images, texts, 0)
    a_01 = send("a_01", a_0, first_hop(a_is_text))
    b_01 = send("b_01", b_0, first_hop(b_is_text))
    near_0 = send("near_0", b_0, other_core)
    rest = after((images, texts), a_0, b_0)
    a_1, b_1 = half(which, *rest, HALF)
    a, b = (a_0, a_1), (b_0, b_1)
    a_sum, = pairs(scalars, Side(a, b, has_own=True))
    b_near, = after((b_1,), a_sum)
    near_1 = send("near_1", b_near, other_core)

    a_1, b_1, a_sum = after((a_1, b_1, a_sum), near_0)
    a_11 = send("a_11", a_1, first_hop(a_is_text))
    b_11 = send("b_11", b_1, first_hop(b_is_text))
    a_01, b_01, a_sum = after((a_01, b_01, a_sum))
    a_x0 = send("a_x0", jnp.where(a_end, a_01, a_0), along(a_is_text))
    b_x0 = send("b_x0", jnp.where(b_end, b_01, b_0), along(b_is_text))
    near_0, near_1, a_sum = after((near_0, near_1, a_sum), a_01, b_01)
    b_sum, = pairs(scalars, Side(b, [*a, near_0, near_1], has_own=True))

    a_01, b_01, b_sum = after((a_01, b_01, b_sum), a_11, b_11)
    a_02 = send("a_02", a_01, second_hop(a_is_text))
    b_02 = send("b_02", b_01, second_hop(b_is_text))
    a_x1 = send("a_x1", jnp.where(a_end, a_11, a_1), along(a_is_text))
    b_x1 = send("b_x1", jnp.where(b_end, b_11, b_1), along(b_is_text))
    far_0 = send("far_0", a_x0, other_core)
    b_sum, = pairs(scalars, Side(b, [a_x0], b_sum))
    a_sum, = pairs(scalars, Side(a, [b_x0, far_0], a_sum))

    a_11, b_11, a_sum, b_sum = after((a_11, b_11, a_sum, b_sum), a_02, b_02)
    a_12 = send("a_12", a_11, second_hop(a_is_text))
    b_12 = send("b_12", b_11, second_hop(b_is_text))
    a_x1, a_sum = after((a_x1, a_sum))
    far_1 = send("far_1", a_x1, other_core)
    sums, = pairs(scalars, Side(b, [a_02, a_x1], b_sum), at=1)
    sums, = pairs(scalars, Side(a, [b_02, b_x1, far_1], a_sum), at=0, stack=sums)

    return tuple(last_pairs(which, scalars, b_12, a_12, images, texts, sums))


def solution(mesh):
    return jax.shard_map(
        body,
        mesh=mesh,
        in_specs=(P(AXES, None), P(AXES, None), P(), P()),
        out_specs=(P(AXES, None), P(AXES, None)),
        check_vma=False,
    )
```

```python
import functools

import jax
import jax.numpy as jnp
from jax import lax
from jax.experimental import pallas as pl
from jax.experimental.pallas import tpu as pltpu
from jax.sharding import PartitionSpec as P

EPSILON = 1e-06
D = 1152
ROWS = 1024
HALF = 512
TILE = 256
AXES = ("grp", "blk")
WIDE = 384
FEW = 32
VMEM_LIMIT = 48 * 1024 * 1024
EDGE_LIMIT = 63 * 1024 * 1024
COST = pl.CostEstimate(flops=0, bytes_accessed=0, transcendentals=0)


def device(z, y, x, c):
    return (((z % 4) * 4 + y % 4) * 4 + x % 4) * 2 + c


def route(target):
    pairs = []
    for z in range(4):
        for y in range(4):
            for x in range(4):
                for c in range(2):
                    pairs.append((device(z, y, x, c), device(*target(z, y, x, c))))
    return pairs


def inner_first(is_text, x):
    return (x >= 2) == is_text


def first_hop(is_text):
    def target(z, y, x, c):
        return (z, y ^ 1 if inner_first(is_text(c), x) else 3 - y, x, c)

    return target


def second_hop(is_text):
    def target(z, y, x, c):
        inner = inner_first(is_text(c), x)
        origin = y ^ 1 if inner else 3 - y
        to = 3 - y if inner else y ^ 1
        if is_text(c):
            z += 1 if origin >= 2 else 0
        else:
            z -= 1 if origin < 2 else 0
        return (z, to, x, c)

    return target


def along(is_text):
    return lambda z, y, x, c: (z, y, x + 1 if is_text(c) else x - 1, c)


def other_core(z, y, x, c):
    return (z, y, x, 1 - c)


def a_is_text(c):
    return c == 1


def b_is_text(c):
    return c == 0


def send(name, value, target):
    with jax.named_scope(name):
        return lax.ppermute(value, AXES, route(target))


def after(values, *others):
    held = lax.optimization_barrier((tuple(values), tuple(others)))
    return held[0]


def scale_of(squares):
    return 1.0 / jnp.sqrt(squares + EPSILON)


def pieces(rows):
    return [slice(start, start + FEW) for start in range(0, rows, FEW)]


def normalized(raw):
    values = raw.astype(jnp.float32)
    scale = scale_of(jnp.sum(values * values, axis=-1, keepdims=True))
    return values * scale, scale


def half_kernel(core, images, texts, a, b):
    for rows in pieces(TILE):
        image_unit = normalized(images[rows, :])[0]
        text_unit = normalized(texts[rows, :])[0]
        a[rows, :] = jnp.where(core[0] == 0, image_unit, text_unit).astype(jnp.bfloat16)
        b[rows, :] = jnp.where(core[0] == 0, text_unit, image_unit).astype(jnp.bfloat16)


def half(core, images, texts, first):
    spec = pl.BlockSpec((TILE, D), lambda i: (i + first // TILE, 0))
    out = pl.BlockSpec((TILE, D), lambda i: (i, 0))
    shape = jax.ShapeDtypeStruct((HALF, D), jnp.bfloat16)
    return pl.pallas_call(
        half_kernel,
        grid=(HALF // TILE,),
        in_specs=[pl.BlockSpec(memory_space=pltpu.SMEM), spec, spec],
        out_specs=[out, out],
        out_shape=[shape, shape],
        compiler_params=pltpu.CompilerParams(vmem_limit_bytes=EDGE_LIMIT),
        cost_estimate=COST,
    )(core, images, texts)


def coefficients(dots, scalars, diagonal_at=None):
    bent = jnp.tanh(dots * scalars[0] + scalars[1])
    if diagonal_at is None:
        return ((bent + 1.0) * scalars[0]).astype(jnp.bfloat16)
    down = lax.broadcasted_iota(jnp.int32, dots.shape, 0)
    across = lax.broadcasted_iota(jnp.int32, dots.shape, 1) + diagonal_at
    return ((bent + jnp.where(across == down, -1.0, 1.0)) * scalars[0]).astype(jnp.bfloat16)


def row_dots(own, paired):
    return lax.dot_general(own, paired, (((1,), (1,)), ((), ())), preferred_element_type=jnp.float32)


class Side:
    def __init__(self, owns, partners, before=None, has_own=False):
        self.owns, self.partners, self.before, self.has_own = owns, partners, before, has_own
        self.count = len(partners)
        self.rows = sum(partner.shape[0] for partner in partners)
        self.steps = self.count + D // WIDE


def columns(part):
    return slice(part * WIDE, (part + 1) * WIDE)


def side_steps(side, first, scalars, owns, partners, before, held, arrived, total, factors):
    step = pl.program_id(0)
    loads = []
    if before is not None:
        loads = [
            pltpu.make_async_copy(before.at[:, columns(part)], held.at[:, columns(part)], arrived.at[part])
            for part in range(D // WIDE)
        ]

        @pl.when(step == 0)
        def _():
            for load in loads:
                load.start()

    base = 0
    for at, partner in enumerate(partners):
        def make(partner=partner, base=base):
            for start in range(0, partner.shape[0], TILE):
                for half_at, own in enumerate(owns):
                    top = half_at * HALF
                    dots = row_dots(own[...], partner[start : start + TILE, :])
                    diagonal_at = base + start - top if side.has_own and base < ROWS else None
                    factors[top : top + own.shape[0], base + start : base + start + TILE] = coefficients(
                        dots, scalars, diagonal_at
                    )

        pl.when(step == first + at)(make)
        base += partner.shape[0]

    for part in range(D // WIDE):
        def add(part=part):
            result = None
            if loads:
                loads[part].wait()
                result = held[:, columns(part)]
            base = 0
            for partner in partners:
                rows = partner.shape[0]
                term = jnp.dot(factors[:, base : base + rows], partner[:, columns(part)], preferred_element_type=jnp.float32)
                result = term if result is None else result + term
                base += rows
            total[...] = result

        pl.when(step == first + side.count + part)(add)


def pairs_kernel(sides, has_stack, scalars, *refs):
    refs = list(refs)
    take = lambda count: [refs.pop(0) for _ in range(count)]
    inputs = [(take(2), take(side.count), take(1)[0] if side.before is not None else None) for side in sides]
    take(has_stack)
    totals = take(len(sides))
    factors = take(1)[0]
    first = 0
    for side, (owns, partners, before), total in zip(sides, inputs, totals):
        held, arrived = take(2) if before is not None else (None, None)
        side_steps(side, first, scalars, owns, partners, before, held, arrived, total, factors)
        first += side.steps


def pairs(scalars, *sides, at=None, stack=None):
    specs, values, out_specs, scratch = [], [], [], []
    first = 0
    for side in sides:
        for value in (*side.owns, *side.partners):
            specs.append(pl.BlockSpec(value.shape, lambda i: (0, 0), pipeline_mode=pl.Buffered(1)))
            values.append(value)
        if side.before is not None:
            specs.append(pl.BlockSpec(memory_space=pl.ANY))
            values.append(side.before)
            scratch += [pltpu.VMEM((ROWS, D), jnp.float32), pltpu.SemaphoreType.DMA((D // WIDE,))]
        begin = first + side.count
        last = D // WIDE - 1
        out_specs.append(pl.BlockSpec((ROWS, WIDE), lambda i, begin=begin: (0, jnp.clip(i - begin, 0, last))))
        first += side.steps
    factors = pltpu.VMEM((ROWS, max(side.rows for side in sides)), jnp.bfloat16)
    shape = jax.ShapeDtypeStruct((ROWS, D), jnp.float32)
    if at is not None:
        shape = jax.ShapeDtypeStruct((2, ROWS, D), jnp.float32)
        out_specs = [pl.BlockSpec((None, ROWS, WIDE), lambda i: (at, 0, jnp.clip(i - sides[0].count, 0, D // WIDE - 1)))]
    aliases = {}
    if stack is not None:
        specs.append(pl.BlockSpec(memory_space=pl.ANY))
        values.append(stack)
        aliases = {len(values): 0}
    return pl.pallas_call(
        functools.partial(pairs_kernel, sides, int(stack is not None)),
        grid=(first,),
        in_specs=[pl.BlockSpec(memory_space=pltpu.SMEM), *specs],
        out_specs=out_specs,
        out_shape=[shape] * len(sides),
        input_output_aliases=aliases,
        scratch_shapes=[factors, *scratch],
        compiler_params=pltpu.CompilerParams(vmem_limit_bytes=VMEM_LIMIT),
        cost_estimate=COST,
    )(scalars, *values)


def last_kernel(core, scalars, a_pair, b_pair, images, texts, image_before, text_before, image_grad, text_grad, pair):
    @pl.when(pl.program_id(0) == 0)
    def _():
        is_zero = core[0] == 0
        pair[0] = jnp.where(is_zero, a_pair[...], b_pair[...])
        pair[1] = jnp.where(is_zero, b_pair[...], a_pair[...])

    for side, (raw, before, grad) in enumerate(((images, image_before, image_grad), (texts, text_before, text_grad))):
        unit, scale = normalized(raw[...])
        own = unit.astype(jnp.bfloat16)
        factor = jnp.concatenate(
            [
                coefficients(row_dots(own, pair[side, start : start + TILE, :]), scalars)
                for start in range(0, a_pair.shape[0], TILE)
            ],
            axis=1,
        )
        total = before[...] + jnp.dot(factor, pair[side], preferred_element_type=jnp.float32)
        inside = jnp.sum(unit * total, axis=-1, keepdims=True)
        grad[...] = (total - unit * inside) * scale


def last_pairs(core, scalars, a_pair, b_pair, images, texts, before):
    spec = pl.BlockSpec((TILE, D), lambda i, core: (i, 0))
    image_before = pl.BlockSpec((None, TILE, D), lambda i, core: (core[0], i, 0))
    text_before = pl.BlockSpec((None, TILE, D), lambda i, core: (1 - core[0], i, 0))
    whole = pl.BlockSpec(a_pair.shape, lambda i, core: (0, 0), pipeline_mode=pl.Buffered(1))
    grad = jax.ShapeDtypeStruct((ROWS, D), jnp.float32)
    return pl.pallas_call(
        last_kernel,
        grid_spec=pltpu.PrefetchScalarGridSpec(
            num_scalar_prefetch=1,
            grid=(ROWS // TILE,),
            in_specs=[
                pl.BlockSpec(memory_space=pltpu.SMEM), whole, whole, spec, spec, image_before, text_before,
            ],
            out_specs=[spec, spec],
            scratch_shapes=[pltpu.VMEM((2, *a_pair.shape), jnp.bfloat16)],
        ),
        out_shape=[grad, grad],
        compiler_params=pltpu.CompilerParams(vmem_limit_bytes=EDGE_LIMIT),
        cost_estimate=COST,
    )(core, scalars, a_pair, b_pair, images, texts, before, before)


def body(images, texts, log_logit_scale, bias):
    scalars = 0.5 * jnp.concatenate([jnp.exp(log_logit_scale), bias])
    index = lax.axis_index(AXES).astype(jnp.int32)
    core = lax.rem(index, 2)
    x = lax.rem(lax.div(index, 2), 4)
    which = jnp.reshape(core, (1,))
    text_end, image_end = x == 3, x == 0
    a_end = jnp.where(core == 0, image_end, text_end)
    b_end = jnp.where(core == 0, text_end, image_end)

    a_0, b_0 = half(which, images, texts, 0)
    a_01 = send("a_01", a_0, first_hop(a_is_text))
    b_01 = send("b_01", b_0, first_hop(b_is_text))
    near_0 = send("near_0", b_0, other_core)
    rest = after((images, texts), a_0, b_0)
    a_1, b_1 = half(which, *rest, HALF)
    a, b = (a_0, a_1), (b_0, b_1)
    a_sum, = pairs(scalars, Side(a, b, has_own=True))
    b_near, = after((b_1,), a_sum)
    near_1 = send("near_1", b_near, other_core)

    a_1, b_1, a_sum = after((a_1, b_1, a_sum), near_0)
    a_11 = send("a_11", a_1, first_hop(a_is_text))
    b_11 = send("b_11", b_1, first_hop(b_is_text))
    a_01, b_01, a_sum = after((a_01, b_01, a_sum))
    a_x0 = send("a_x0", jnp.where(a_end, a_01, a_0), along(a_is_text))
    b_x0 = send("b_x0", jnp.where(b_end, b_01, b_0), along(b_is_text))
    near_0, near_1, a_sum = after((near_0, near_1, a_sum), a_01, b_01)
    b_sum, = pairs(scalars, Side(b, [*a, near_0, near_1], has_own=True))

    a_01, b_sum = after((a_01, b_sum))
    b_01, b_sum = after((b_01, b_sum), a_11, b_11)
    a_02 = send("a_02", a_01, second_hop(a_is_text))
    b_02 = send("b_02", b_01, second_hop(b_is_text))
    a_x1 = send("a_x1", jnp.where(a_end, a_11, a_1), along(a_is_text))
    b_x1 = send("b_x1", jnp.where(b_end, b_11, b_1), along(b_is_text))
    far_0 = send("far_0", a_x0, other_core)
    b_sum, = pairs(scalars, Side(b, [a_x0], b_sum))
    a_sum, = pairs(scalars, Side(a, [b_x0, far_0], a_sum))

    a_11, a_sum, b_sum = after((a_11, a_sum, b_sum))
    b_11, a_sum, b_sum = after((b_11, a_sum, b_sum), a_02, b_02)
    a_12 = send("a_12", a_11, second_hop(a_is_text))
    b_12 = send("b_12", b_11, second_hop(b_is_text))
    a_x1, a_sum = after((a_x1, a_sum))
    far_1 = send("far_1", a_x1, other_core)
    sums, = pairs(scalars, Side(b, [a_02, a_x1], b_sum), at=1)
    sums, = pairs(scalars, Side(a, [b_02, b_x1, far_1], a_sum), at=0, stack=sums)

    return tuple(last_pairs(which, scalars, b_12, a_12, images, texts, sums))


def solution(mesh):
    return jax.shard_map(
        body,
        mesh=mesh,
        in_specs=(P(AXES, None), P(AXES, None), P(), P()),
        out_specs=(P(AXES, None), P(AXES, None)),
        check_vma=False,
    )
```

```python
import functools

import jax
import jax.numpy as jnp
from jax import lax
from jax.experimental import pallas as pl
from jax.experimental.pallas import tpu as pltpu
from jax.sharding import PartitionSpec as P

EPSILON = 1e-06
D = 1152
ROWS = 1024
HALF = 512
TILE = 256
TALL = 512
AXES = ("grp", "blk")
WIDE = 384
FEW = 32
VMEM_LIMIT = 48 * 1024 * 1024
EDGE_LIMIT = 63 * 1024 * 1024
COST = pl.CostEstimate(flops=0, bytes_accessed=0, transcendentals=0)


def device(z, y, x, c):
    return (((z % 4) * 4 + y % 4) * 4 + x % 4) * 2 + c


def route(target):
    pairs = []
    for z in range(4):
        for y in range(4):
            for x in range(4):
                for c in range(2):
                    pairs.append((device(z, y, x, c), device(*target(z, y, x, c))))
    return pairs


def inner_first(is_text, x):
    return (x >= 2) == is_text


def first_hop(is_text):
    def target(z, y, x, c):
        return (z, y ^ 1 if inner_first(is_text(c), x) else 3 - y, x, c)

    return target


def second_hop(is_text):
    def target(z, y, x, c):
        inner = inner_first(is_text(c), x)
        origin = y ^ 1 if inner else 3 - y
        to = 3 - y if inner else y ^ 1
        if is_text(c):
            z += 1 if origin >= 2 else 0
        else:
            z -= 1 if origin < 2 else 0
        return (z, to, x, c)

    return target


def along(is_text):
    return lambda z, y, x, c: (z, y, x + 1 if is_text(c) else x - 1, c)


def other_core(z, y, x, c):
    return (z, y, x, 1 - c)


def a_is_text(c):
    return c == 1


def b_is_text(c):
    return c == 0


def send(name, value, target):
    with jax.named_scope(name):
        return lax.ppermute(value, AXES, route(target))


def after(values, *others):
    held = lax.optimization_barrier((tuple(values), tuple(others)))
    return held[0]


def scale_of(squares):
    return 1.0 / jnp.sqrt(squares + EPSILON)


def pieces(rows):
    return [slice(start, start + FEW) for start in range(0, rows, FEW)]


def normalized(raw):
    values = raw.astype(jnp.float32)
    scale = scale_of(jnp.sum(values * values, axis=-1, keepdims=True))
    return values * scale, scale


def half_kernel(core, images, texts, a, b):
    for rows in pieces(TILE):
        image_unit = normalized(images[rows, :])[0]
        text_unit = normalized(texts[rows, :])[0]
        a[rows, :] = jnp.where(core[0] == 0, image_unit, text_unit).astype(jnp.bfloat16)
        b[rows, :] = jnp.where(core[0] == 0, text_unit, image_unit).astype(jnp.bfloat16)


def half(core, images, texts, first):
    spec = pl.BlockSpec((TILE, D), lambda i: (i + first // TILE, 0))
    out = pl.BlockSpec((TILE, D), lambda i: (i, 0))
    shape = jax.ShapeDtypeStruct((HALF, D), jnp.bfloat16)
    return pl.pallas_call(
        half_kernel,
        grid=(HALF // TILE,),
        in_specs=[pl.BlockSpec(memory_space=pltpu.SMEM), spec, spec],
        out_specs=[out, out],
        out_shape=[shape, shape],
        compiler_params=pltpu.CompilerParams(vmem_limit_bytes=EDGE_LIMIT),
        cost_estimate=COST,
    )(core, images, texts)


def coefficients(dots, scalars, diagonal_at=None):
    bent = jnp.tanh(dots * scalars[0] + scalars[1])
    if diagonal_at is None:
        return ((bent + 1.0) * scalars[0]).astype(jnp.bfloat16)
    down = lax.broadcasted_iota(jnp.int32, dots.shape, 0)
    across = lax.broadcasted_iota(jnp.int32, dots.shape, 1) + diagonal_at
    return ((bent + jnp.where(across == down, -1.0, 1.0)) * scalars[0]).astype(jnp.bfloat16)


def row_dots(own, paired):
    return lax.dot_general(own, paired, (((1,), (1,)), ((), ())), preferred_element_type=jnp.float32)


class Side:
    def __init__(self, owns, partners, before=None, has_own=False):
        self.owns, self.partners, self.before, self.has_own = owns, partners, before, has_own
        self.count = len(partners)
        self.rows = sum(partner.shape[0] for partner in partners)
        self.steps = self.count + D // WIDE


def columns(part):
    return slice(part * WIDE, (part + 1) * WIDE)


def side_steps(side, first, scalars, owns, partners, before, held, arrived, total, factors):
    step = pl.program_id(0)
    loads = []
    if before is not None:
        loads = [
            pltpu.make_async_copy(before.at[:, columns(part)], held.at[:, columns(part)], arrived.at[part])
            for part in range(D // WIDE)
        ]

        @pl.when(step == 0)
        def _():
            for load in loads:
                load.start()

    base = 0
    for at, partner in enumerate(partners):
        def make(partner=partner, base=base):
            for start in range(0, partner.shape[0], TILE):
                for half_at, own in enumerate(owns):
                    top = half_at * HALF
                    dots = row_dots(own[...], partner[start : start + TILE, :])
                    diagonal_at = base + start - top if side.has_own and base < ROWS else None
                    factors[top : top + own.shape[0], base + start : base + start + TILE] = coefficients(
                        dots, scalars, diagonal_at
                    )

        pl.when(step == first + at)(make)
        base += partner.shape[0]

    for part in range(D // WIDE):
        def add(part=part):
            result = None
            if loads:
                loads[part].wait()
                result = held[:, columns(part)]
            base = 0
            for partner in partners:
                rows = partner.shape[0]
                term = jnp.dot(factors[:, base : base + rows], partner[:, columns(part)], preferred_element_type=jnp.float32)
                result = term if result is None else result + term
                base += rows
            total[...] = result

        pl.when(step == first + side.count + part)(add)


def pairs_kernel(sides, has_stack, scalars, *refs):
    refs = list(refs)
    take = lambda count: [refs.pop(0) for _ in range(count)]
    inputs = [(take(2), take(side.count), take(1)[0] if side.before is not None else None) for side in sides]
    take(has_stack)
    totals = take(len(sides))
    factors = take(1)[0]
    first = 0
    for side, (owns, partners, before), total in zip(sides, inputs, totals):
        held, arrived = take(2) if before is not None else (None, None)
        side_steps(side, first, scalars, owns, partners, before, held, arrived, total, factors)
        first += side.steps


def pairs(scalars, *sides, at=None, stack=None):
    specs, values, out_specs, scratch = [], [], [], []
    first = 0
    for side in sides:
        for value in (*side.owns, *side.partners):
            specs.append(pl.BlockSpec(value.shape, lambda i: (0, 0), pipeline_mode=pl.Buffered(1)))
            values.append(value)
        if side.before is not None:
            specs.append(pl.BlockSpec(memory_space=pl.ANY))
            values.append(side.before)
            scratch += [pltpu.VMEM((ROWS, D), jnp.float32), pltpu.SemaphoreType.DMA((D // WIDE,))]
        begin = first + side.count
        last = D // WIDE - 1
        out_specs.append(pl.BlockSpec((ROWS, WIDE), lambda i, begin=begin: (0, jnp.clip(i - begin, 0, last))))
        first += side.steps
    factors = pltpu.VMEM((ROWS, max(side.rows for side in sides)), jnp.bfloat16)
    shape = jax.ShapeDtypeStruct((ROWS, D), jnp.float32)
    if at is not None:
        shape = jax.ShapeDtypeStruct((2, ROWS, D), jnp.float32)
        out_specs = [pl.BlockSpec((None, ROWS, WIDE), lambda i: (at, 0, jnp.clip(i - sides[0].count, 0, D // WIDE - 1)))]
    aliases = {}
    if stack is not None:
        specs.append(pl.BlockSpec(memory_space=pl.ANY))
        values.append(stack)
        aliases = {len(values): 0}
    return pl.pallas_call(
        functools.partial(pairs_kernel, sides, int(stack is not None)),
        grid=(first,),
        in_specs=[pl.BlockSpec(memory_space=pltpu.SMEM), *specs],
        out_specs=out_specs,
        out_shape=[shape] * len(sides),
        input_output_aliases=aliases,
        scratch_shapes=[factors, *scratch],
        compiler_params=pltpu.CompilerParams(vmem_limit_bytes=VMEM_LIMIT),
        cost_estimate=COST,
    )(scalars, *values)


def last_kernel(core, scalars, a_pair, b_pair, images, texts, image_before, text_before, image_grad, text_grad, pair):
    @pl.when(pl.program_id(0) == 0)
    def _():
        is_zero = core[0] == 0
        pair[0] = jnp.where(is_zero, a_pair[...], b_pair[...])
        pair[1] = jnp.where(is_zero, b_pair[...], a_pair[...])

    for side, (raw, before, grad) in enumerate(((images, image_before, image_grad), (texts, text_before, text_grad))):
        unit, scale = normalized(raw[...])
        own = unit.astype(jnp.bfloat16)
        factor = jnp.concatenate(
            [
                coefficients(row_dots(own, pair[side, start : start + TILE, :]), scalars)
                for start in range(0, a_pair.shape[0], TILE)
            ],
            axis=1,
        )
        total = before[...] + jnp.dot(factor, pair[side], preferred_element_type=jnp.float32)
        inside = jnp.sum(unit * total, axis=-1, keepdims=True)
        grad[...] = (total - unit * inside) * scale


def last_pairs(core, scalars, a_pair, b_pair, images, texts, before):
    spec = pl.BlockSpec((TALL, D), lambda i, core: (i, 0))
    image_before = pl.BlockSpec((None, TALL, D), lambda i, core: (core[0], i, 0))
    text_before = pl.BlockSpec((None, TALL, D), lambda i, core: (1 - core[0], i, 0))
    whole = pl.BlockSpec(a_pair.shape, lambda i, core: (0, 0), pipeline_mode=pl.Buffered(1))
    grad = jax.ShapeDtypeStruct((ROWS, D), jnp.float32)
    return pl.pallas_call(
        last_kernel,
        grid_spec=pltpu.PrefetchScalarGridSpec(
            num_scalar_prefetch=1,
            grid=(ROWS // TALL,),
            in_specs=[
                pl.BlockSpec(memory_space=pltpu.SMEM), whole, whole, spec, spec, image_before, text_before,
            ],
            out_specs=[spec, spec],
            scratch_shapes=[pltpu.VMEM((2, *a_pair.shape), jnp.bfloat16)],
        ),
        out_shape=[grad, grad],
        compiler_params=pltpu.CompilerParams(vmem_limit_bytes=EDGE_LIMIT),
        cost_estimate=COST,
    )(core, scalars, a_pair, b_pair, images, texts, before, before)


def body(images, texts, log_logit_scale, bias):
    scalars = 0.5 * jnp.concatenate([jnp.exp(log_logit_scale), bias])
    index = lax.axis_index(AXES).astype(jnp.int32)
    core = lax.rem(index, 2)
    x = lax.rem(lax.div(index, 2), 4)
    which = jnp.reshape(core, (1,))
    text_end, image_end = x == 3, x == 0
    a_end = jnp.where(core == 0, image_end, text_end)
    b_end = jnp.where(core == 0, text_end, image_end)

    a_0, b_0 = half(which, images, texts, 0)
    a_01 = send("a_01", a_0, first_hop(a_is_text))
    b_01 = send("b_01", b_0, first_hop(b_is_text))
    near_0 = send("near_0", b_0, other_core)
    rest = after((images, texts), a_0, b_0)
    a_1, b_1 = half(which, *rest, HALF)
    a, b = (a_0, a_1), (b_0, b_1)
    a_sum, = pairs(scalars, Side(a, b, has_own=True))
    b_near, = after((b_1,), a_sum)
    near_1 = send("near_1", b_near, other_core)

    a_1, b_1, a_sum = after((a_1, b_1, a_sum), near_0)
    a_11 = send("a_11", a_1, first_hop(a_is_text))
    b_11 = send("b_11", b_1, first_hop(b_is_text))
    a_01, b_01, a_sum = after((a_01, b_01, a_sum))
    a_x0 = send("a_x0", jnp.where(a_end, a_01, a_0), along(a_is_text))
    b_x0 = send("b_x0", jnp.where(b_end, b_01, b_0), along(b_is_text))
    near_0, near_1, a_sum = after((near_0, near_1, a_sum), a_01, b_01)
    b_sum, = pairs(scalars, Side(b, [*a, near_0, near_1], has_own=True))

    a_01, b_sum = after((a_01, b_sum))
    b_01, b_sum = after((b_01, b_sum), a_11, b_11)
    a_02 = send("a_02", a_01, second_hop(a_is_text))
    b_02 = send("b_02", b_01, second_hop(b_is_text))
    a_x1 = send("a_x1", jnp.where(a_end, a_11, a_1), along(a_is_text))
    b_x1 = send("b_x1", jnp.where(b_end, b_11, b_1), along(b_is_text))
    far_0 = send("far_0", a_x0, other_core)
    b_sum, = pairs(scalars, Side(b, [a_x0], b_sum))
    a_sum, = pairs(scalars, Side(a, [b_x0, far_0], a_sum))

    a_11, a_sum, b_sum = after((a_11, a_sum, b_sum))
    b_11, a_sum, b_sum = after((b_11, a_sum, b_sum), a_02, b_02)
    a_12 = send("a_12", a_11, second_hop(a_is_text))
    b_12 = send("b_12", b_11, second_hop(b_is_text))
    a_x1, a_sum = after((a_x1, a_sum))
    far_1 = send("far_1", a_x1, other_core)
    sums, = pairs(scalars, Side(b, [a_02, a_x1], b_sum), at=1)
    sums, = pairs(scalars, Side(a, [b_02, b_x1, far_1], a_sum), at=0, stack=sums)

    return tuple(last_pairs(which, scalars, b_12, a_12, images, texts, sums))


def solution(mesh):
    return jax.shard_map(
        body,
        mesh=mesh,
        in_specs=(P(AXES, None), P(AXES, None), P(), P()),
        out_specs=(P(AXES, None), P(AXES, None)),
        check_vma=False,
    )
```

```python
import functools

import jax
import jax.numpy as jnp
from jax import lax
from jax.experimental import pallas as pl
from jax.experimental.pallas import tpu as pltpu
from jax.sharding import PartitionSpec as P

EPSILON = 1e-06
D = 1152
ROWS = 1024
HALF = 512
TILE = 256
AXES = ("grp", "blk")
WIDE = 384
FEW = 32
VMEM_LIMIT = 48 * 1024 * 1024
EDGE_LIMIT = 63 * 1024 * 1024
COST = pl.CostEstimate(flops=0, bytes_accessed=0, transcendentals=0)


def device(z, y, x, c):
    return (((z % 4) * 4 + y % 4) * 4 + x % 4) * 2 + c


def route(target):
    pairs = []
    for z in range(4):
        for y in range(4):
            for x in range(4):
                for c in range(2):
                    pairs.append((device(z, y, x, c), device(*target(z, y, x, c))))
    return pairs


def inner_first(is_text, x):
    return (x >= 2) == is_text


def first_hop(is_text):
    def target(z, y, x, c):
        return (z, y ^ 1 if inner_first(is_text(c), x) else 3 - y, x, c)

    return target


def second_hop(is_text):
    def target(z, y, x, c):
        inner = inner_first(is_text(c), x)
        origin = y ^ 1 if inner else 3 - y
        to = 3 - y if inner else y ^ 1
        if is_text(c):
            z += 1 if origin >= 2 else 0
        else:
            z -= 1 if origin < 2 else 0
        return (z, to, x, c)

    return target


def along(is_text):
    return lambda z, y, x, c: (z, y, x + 1 if is_text(c) else x - 1, c)


def other_core(z, y, x, c):
    return (z, y, x, 1 - c)


def a_is_text(c):
    return c == 1


def b_is_text(c):
    return c == 0


def send(name, value, target):
    with jax.named_scope(name):
        return lax.ppermute(value, AXES, route(target))


def after(values, *others):
    held = lax.optimization_barrier((tuple(values), tuple(others)))
    return held[0]


def scale_of(squares):
    return 1.0 / jnp.sqrt(squares + EPSILON)


def pieces(rows):
    return [slice(start, start + FEW) for start in range(0, rows, FEW)]


def normalized(raw):
    values = raw.astype(jnp.float32)
    scale = scale_of(jnp.sum(values * values, axis=-1, keepdims=True))
    return values * scale, scale


def half_kernel(core, images, texts, a, b):
    for rows in pieces(TILE):
        image_unit = normalized(images[rows, :])[0]
        text_unit = normalized(texts[rows, :])[0]
        a[rows, :] = jnp.where(core[0] == 0, image_unit, text_unit).astype(jnp.bfloat16)
        b[rows, :] = jnp.where(core[0] == 0, text_unit, image_unit).astype(jnp.bfloat16)


def half(core, images, texts, first):
    spec = pl.BlockSpec((TILE, D), lambda i: (i + first // TILE, 0))
    out = pl.BlockSpec((TILE, D), lambda i: (i, 0))
    shape = jax.ShapeDtypeStruct((HALF, D), jnp.bfloat16)
    return pl.pallas_call(
        half_kernel,
        grid=(HALF // TILE,),
        in_specs=[pl.BlockSpec(memory_space=pltpu.SMEM), spec, spec],
        out_specs=[out, out],
        out_shape=[shape, shape],
        compiler_params=pltpu.CompilerParams(vmem_limit_bytes=EDGE_LIMIT),
        cost_estimate=COST,
    )(core, images, texts)


def coefficients(dots, scalars, diagonal_at=None):
    bent = jnp.tanh(dots * scalars[0] + scalars[1])
    if diagonal_at is None:
        return ((bent + 1.0) * scalars[0]).astype(jnp.bfloat16)
    down = lax.broadcasted_iota(jnp.int32, dots.shape, 0)
    across = lax.broadcasted_iota(jnp.int32, dots.shape, 1) + diagonal_at
    return ((bent + jnp.where(across == down, -1.0, 1.0)) * scalars[0]).astype(jnp.bfloat16)


def row_dots(own, paired):
    return lax.dot_general(own, paired, (((1,), (1,)), ((), ())), preferred_element_type=jnp.float32)


class Side:
    def __init__(self, owns, partners, before=None, has_own=False):
        self.owns, self.partners, self.before, self.has_own = owns, partners, before, has_own
        self.count = len(partners)
        self.rows = sum(partner.shape[0] for partner in partners)
        self.steps = self.count + D // WIDE


def columns(part):
    return slice(part * WIDE, (part + 1) * WIDE)


def side_steps(side, first, scalars, owns, partners, before, held, arrived, total, factors):
    step = pl.program_id(0)
    loads = []
    if before is not None:
        loads = [
            pltpu.make_async_copy(before.at[:, columns(part)], held.at[:, columns(part)], arrived.at[part])
            for part in range(D // WIDE)
        ]

        @pl.when(step == 0)
        def _():
            for load in loads:
                load.start()

    base = 0
    for at, partner in enumerate(partners):
        def make(partner=partner, base=base):
            for start in range(0, partner.shape[0], TILE):
                for half_at, own in enumerate(owns):
                    top = half_at * HALF
                    dots = row_dots(own[...], partner[start : start + TILE, :])
                    diagonal_at = base + start - top if side.has_own and base < ROWS else None
                    factors[top : top + own.shape[0], base + start : base + start + TILE] = coefficients(
                        dots, scalars, diagonal_at
                    )

        pl.when(step == first + at)(make)
        base += partner.shape[0]

    for part in range(D // WIDE):
        def add(part=part):
            result = None
            if loads:
                loads[part].wait()
                result = held[:, columns(part)]
            base = 0
            for partner in partners:
                rows = partner.shape[0]
                term = jnp.dot(factors[:, base : base + rows], partner[:, columns(part)], preferred_element_type=jnp.float32)
                result = term if result is None else result + term
                base += rows
            total[...] = result

        pl.when(step == first + side.count + part)(add)


def pairs_kernel(sides, has_stack, scalars, *refs):
    refs = list(refs)
    take = lambda count: [refs.pop(0) for _ in range(count)]
    inputs = [(take(2), take(side.count), take(1)[0] if side.before is not None else None) for side in sides]
    take(has_stack)
    totals = take(len(sides))
    factors = take(1)[0]
    first = 0
    for side, (owns, partners, before), total in zip(sides, inputs, totals):
        held, arrived = take(2) if before is not None else (None, None)
        side_steps(side, first, scalars, owns, partners, before, held, arrived, total, factors)
        first += side.steps


def pairs(scalars, *sides, at=None, stack=None):
    specs, values, out_specs, scratch = [], [], [], []
    first = 0
    for side in sides:
        for value in (*side.owns, *side.partners):
            specs.append(pl.BlockSpec(value.shape, lambda i: (0, 0), pipeline_mode=pl.Buffered(1)))
            values.append(value)
        if side.before is not None:
            specs.append(pl.BlockSpec(memory_space=pl.ANY))
            values.append(side.before)
            scratch += [pltpu.VMEM((ROWS, D), jnp.float32), pltpu.SemaphoreType.DMA((D // WIDE,))]
        begin = first + side.count
        last = D // WIDE - 1
        out_specs.append(pl.BlockSpec((ROWS, WIDE), lambda i, begin=begin: (0, jnp.clip(i - begin, 0, last))))
        first += side.steps
    factors = pltpu.VMEM((ROWS, max(side.rows for side in sides)), jnp.bfloat16)
    shape = jax.ShapeDtypeStruct((ROWS, D), jnp.float32)
    if at is not None:
        shape = jax.ShapeDtypeStruct((2, ROWS, D), jnp.float32)
        out_specs = [pl.BlockSpec((None, ROWS, WIDE), lambda i: (at, 0, jnp.clip(i - sides[0].count, 0, D // WIDE - 1)))]
    aliases = {}
    if stack is not None:
        specs.append(pl.BlockSpec(memory_space=pl.ANY))
        values.append(stack)
        aliases = {len(values): 0}
    return pl.pallas_call(
        functools.partial(pairs_kernel, sides, int(stack is not None)),
        grid=(first,),
        in_specs=[pl.BlockSpec(memory_space=pltpu.SMEM), *specs],
        out_specs=out_specs,
        out_shape=[shape] * len(sides),
        input_output_aliases=aliases,
        scratch_shapes=[factors, *scratch],
        compiler_params=pltpu.CompilerParams(vmem_limit_bytes=VMEM_LIMIT),
        cost_estimate=COST,
    )(scalars, *values)


def last_kernel(core, scalars, a_pair, b_pair, images, texts, image_before, text_before, image_grad, text_grad, pair):
    @pl.when(pl.program_id(0) == 0)
    def _():
        is_zero = core[0] == 0
        pair[0] = jnp.where(is_zero, a_pair[...], b_pair[...])
        pair[1] = jnp.where(is_zero, b_pair[...], a_pair[...])

    for side, (raw, before, grad) in enumerate(((images, image_before, image_grad), (texts, text_before, text_grad))):
        unit, scale = normalized(raw[...])
        own = unit.astype(jnp.bfloat16)
        factor = jnp.concatenate(
            [
                coefficients(row_dots(own, pair[side, start : start + TILE, :]), scalars)
                for start in range(0, a_pair.shape[0], TILE)
            ],
            axis=1,
        )
        total = before[...] + jnp.dot(factor, pair[side], preferred_element_type=jnp.float32)
        inside = jnp.sum(unit * total, axis=-1, keepdims=True)
        grad[...] = (total - unit * inside) * scale


def last_pairs(core, scalars, a_pair, b_pair, images, texts, before):
    spec = pl.BlockSpec((TILE, D), lambda i, core: (i, 0))
    image_before = pl.BlockSpec((None, TILE, D), lambda i, core: (core[0], i, 0))
    text_before = pl.BlockSpec((None, TILE, D), lambda i, core: (1 - core[0], i, 0))
    whole = pl.BlockSpec(a_pair.shape, lambda i, core: (0, 0), pipeline_mode=pl.Buffered(1))
    grad = jax.ShapeDtypeStruct((ROWS, D), jnp.float32)
    return pl.pallas_call(
        last_kernel,
        grid_spec=pltpu.PrefetchScalarGridSpec(
            num_scalar_prefetch=1,
            grid=(ROWS // TILE,),
            in_specs=[
                pl.BlockSpec(memory_space=pltpu.SMEM), whole, whole, spec, spec, image_before, text_before,
            ],
            out_specs=[spec, spec],
            scratch_shapes=[pltpu.VMEM((2, *a_pair.shape), jnp.bfloat16)],
        ),
        out_shape=[grad, grad],
        compiler_params=pltpu.CompilerParams(vmem_limit_bytes=EDGE_LIMIT),
        cost_estimate=COST,
    )(core, scalars, a_pair, b_pair, images, texts, before, before)


def body(images, texts, log_logit_scale, bias):
    scalars = 0.5 * jnp.concatenate([jnp.exp(log_logit_scale), bias])
    index = lax.axis_index(AXES).astype(jnp.int32)
    core = lax.rem(index, 2)
    x = lax.rem(lax.div(index, 2), 4)
    which = jnp.reshape(core, (1,))
    text_end, image_end = x == 3, x == 0
    a_end = jnp.where(core == 0, image_end, text_end)
    b_end = jnp.where(core == 0, text_end, image_end)

    a_0, b_0 = half(which, images, texts, 0)
    a_01 = send("a_01", a_0, first_hop(a_is_text))
    b_01 = send("b_01", b_0, first_hop(b_is_text))
    near_0 = send("near_0", b_0, other_core)
    rest = after((images, texts), a_0, b_0)
    a_1, b_1 = half(which, *rest, HALF)
    a, b = (a_0, a_1), (b_0, b_1)
    a_sum, = pairs(scalars, Side(a, b, has_own=True))
    b_near, = after((b_1,), a_sum)
    near_1 = send("near_1", b_near, other_core)

    a_1, b_1, a_sum = after((a_1, b_1, a_sum), near_0)
    a_11 = send("a_11", a_1, first_hop(a_is_text))
    b_11 = send("b_11", b_1, first_hop(b_is_text))
    a_01, b_01, a_sum = after((a_01, b_01, a_sum))
    a_x0 = send("a_x0", jnp.where(a_end, a_01, a_0), along(a_is_text))
    b_x0 = send("b_x0", jnp.where(b_end, b_01, b_0), along(b_is_text))
    near_0, near_1, a_sum = after((near_0, near_1, a_sum), a_01, b_01)
    b_sum, = pairs(scalars, Side(b, [*a, near_0, near_1], has_own=True))

    a_01, b_sum = after((a_01, b_sum))
    b_01, b_sum = after((b_01, b_sum), a_11, b_11)
    a_02 = send("a_02", a_01, second_hop(a_is_text))
    b_02 = send("b_02", b_01, second_hop(b_is_text))
    a_x1 = send("a_x1", jnp.where(a_end, a_11, a_1), along(a_is_text))
    b_x1 = send("b_x1", jnp.where(b_end, b_11, b_1), along(b_is_text))
    far_0 = send("far_0", a_x0, other_core)
    b_sum, = pairs(scalars, Side(b, [a_x0], b_sum))
    a_sum, = pairs(scalars, Side(a, [b_x0, far_0], a_sum))

    a_11, a_sum, b_sum = after((a_11, a_sum, b_sum))
    b_11, a_sum, b_sum = after((b_11, a_sum, b_sum), a_02, b_02)
    a_12 = send("a_12", a_11, second_hop(a_is_text))
    a_far, = after((a_x1,), a_02, b_02)
    far_1 = send("far_1", a_far, other_core)
    b_12 = send("b_12", b_11, second_hop(b_is_text))
    sums, = pairs(scalars, Side(b, [a_02, a_x1], b_sum), at=1)
    sums, = pairs(scalars, Side(a, [b_02, b_x1, far_1], a_sum), at=0, stack=sums)

    return tuple(last_pairs(which, scalars, b_12, a_12, images, texts, sums))


def solution(mesh):
    return jax.shard_map(
        body,
        mesh=mesh,
        in_specs=(P(AXES, None), P(AXES, None), P(), P()),
        out_specs=(P(AXES, None), P(AXES, None)),
        check_vma=False,
    )
```
